32 devices in a mesh: space: 8 (over y, x, core), snap: 4 (over z).
Axes of the slice: x: 2, y: 2, z: 4, core: 2. Of those that a mesh axis runs over, the one named last changes fastest.
Arguments:
- snapshots: bfloat16 [8192, 2048], P('space', 'snap'), may hold values from -6 to 6
- eigen_vectors: bfloat16 [2048, 512], replicated, may hold values from -0.125 to 0.125
- singular: float32 [512], replicated, as said below
Outputs:
- pod_modes: bfloat16 [8192, 512], P(('space', 'snap'))
- reduced_operator: float32 [512, 512], replicated
The draws below stay inside these ranges and needn't reach their ends.
Inputs may be any that keep to these rules, and one draw needn't show every extreme that they name: `singular`: every entry lies between a third of and three times the fourth root of 8192.
All inputs are finite; a program needn't handle non-finite values.
Results may differ from the reference program's by a relative error of at most 0.002.
Values may be sent and summed in bfloat16 or wider, within the bound.
A program may use at most 64 MiB of HBM per device.

```python
import math
import jax
import jax.numpy as jnp
from jax import lax

ROWS_DEV = 1024
RANK = 512
POINTS = 8192
SNAPS = 2048
N_SPACE = 8


def draw_singular(key, part):
    key = jax.random.fold_in(key, 7)
    center = float(POINTS) ** 0.25
    spread = jax.random.uniform(key, (RANK,), jnp.float32, -1.0, 1.0)
    values = center * jnp.exp(math.log(3.0) * spread)
    return values.astype(jnp.float32)


def level_of(key, dims, pieces, smallest, high):
    factor_of, own = 1.0, jax.random.fold_in(key, 6)
    for dim, shards_of in pieces:
        heights = jnp.exp(jax.random.uniform(jax.random.fold_in(own, dim), (shards_of,), jnp.float32, smallest / len(pieces), high / len(pieces)))
        factor_of = factor_of * jnp.repeat(heights, dims[dim] // shards_of).reshape([-1 if axis == dim else 1 for axis in range(len(dims))])
    return factor_of


def scatter_about(stream_key, shape, scale, most, cuts=(), dtype=jnp.bfloat16):
    level = level_of(stream_key, shape, cuts, -0.22, 0.18) if cuts else 1.0
    result = jax.random.normal(stream_key, shape, jnp.float32) * scale * level
    return jnp.minimum(jnp.maximum(result, -most), most).astype(dtype)


def setup_inputs(seed: int = 0) -> dict:
    streams_of = jax.random.split(jax.random.key(seed), 4)
    return {
        "snapshots": scatter_about(streams_of[0], (POINTS, SNAPS), 1.0, 6.0, ((0, 8), (1, 4))),
        "eigen_vectors": scatter_about(streams_of[1], (SNAPS, RANK), SNAPS ** -0.5, 0.125),
        "singular": draw_singular(jax.random.fold_in(streams_of[3], 71), 0),
    }


def reference(snapshots, eigen_vectors, singular):
    blocks = snapshots.reshape(N_SPACE, ROWS_DEV, SNAPS)

    def one_block(total, block):
        advanced = jnp.concatenate([block[:, 1:], block[:, :1]], axis=1)
        projected = jnp.dot(block, eigen_vectors, preferred_element_type=jnp.float32)
        forward = jnp.dot(advanced, eigen_vectors, preferred_element_type=jnp.float32)
        modes = (projected / singular[None, :]).astype(jnp.bfloat16)
        pushed = (forward / singular[None, :]).astype(jnp.bfloat16)
        term = lax.dot_general(modes, pushed, (((0,), (0,)), ((), ())), preferred_element_type=jnp.float32)
        return total + term, modes

    start = jnp.zeros((RANK, RANK), jnp.float32)
    reduced_operator, modes = lax.scan(one_block, start, blocks)
    return modes.reshape(POINTS, RANK), reduced_operator
```

```python
import functools

import jax
import jax.numpy as jnp
from jax import lax
from jax.experimental import pallas as pl
from jax.experimental.pallas import tpu as pltpu
from jax.sharding import PartitionSpec as P

MESH = pl.DeviceIdType.MESH
F32, BF16 = jnp.float32, jnp.bfloat16
PLANE = 8


def shift_vectors(vectors, snaps, rank):
    rows = 64

    def one(i, above):
        at = pl.ds(pl.multiple_of(i * rows, rows), rows)
        chunk = vectors[at, :rank].astype(F32)
        moved = pltpu.roll(chunk, 1, 0)
        first = lax.broadcasted_iota(jnp.int32, chunk.shape, 0) == 0
        vectors[at, rank:] = jnp.where(first, above, moved).astype(BF16)
        return chunk[rows - 1 :, :]

    last = vectors[snaps - 16 :, :rank].astype(F32)[15:, :]
    lax.fori_loop(0, snaps // rows, one, last)


def kernel(sizes, x_hbm, e_hbm, s_ref, modes_hbm, op_hbm, *scratch):
    n_space, n_snap, groups, fused = sizes
    (xbuf, vectors, modes, e_sem, x_send, x_recv, own_sem, m_sem) = scratch[:8]
    space, snap = lax.axis_index("space"), lax.axis_index("snap")
    rows, rank = modes.shape
    cols = x_hbm.shape[1]
    snaps = cols * n_snap
    piece = rows // groups

    load_e = pltpu.make_async_copy(e_hbm, vectors.at[:, :rank], e_sem)
    load_e.start()
    own = pltpu.make_async_copy(
        x_hbm.at[pl.ds(pl.multiple_of(snap * rows, rows), rows), :],
        xbuf.at[:, pl.ds(pl.multiple_of(snap * cols, cols), cols)],
        own_sem,
    )
    own.start()

    barrier = pltpu.get_barrier_semaphore()
    for j in range(1, n_snap):
        pl.semaphore_signal(
            barrier, inc=1, device_id=(space, lax.rem(snap + j, n_snap)), device_id_type=MESH
        )
    if fused:
        for j in range(1, n_space):
            pl.semaphore_signal(
                barrier, inc=1, device_id=(lax.rem(space + j, n_space), snap), device_id_type=MESH
            )
    pl.semaphore_wait(barrier, n_snap - 1 + (n_space - 1 if fused else 0))

    def block_copy(g, j):
        to = lax.rem(snap + j, n_snap)
        return pltpu.make_async_remote_copy(
            src_ref=x_hbm.at[pl.ds(pl.multiple_of(to * rows + g * piece, piece), piece), :],
            dst_ref=xbuf.at[
                pl.ds(pl.multiple_of(g * piece, piece), piece),
                pl.ds(pl.multiple_of(snap * cols, cols), cols),
            ],
            send_sem=x_send.at[g, j],
            recv_sem=x_recv.at[g, j],
            device_id=(space, to),
            device_id_type=MESH,
        )

    order = sorted(range(1, n_snap), key=lambda j: -min(j, n_snap - j))

    def send_blocks(g, _):
        for j in order:
            block_copy(g, j).start()
        return _

    lax.fori_loop(0, groups, send_blocks, 0)

    load_e.wait()
    shift_vectors(vectors, snaps, rank)
    own.wait()

    def project(g):
        at = pl.ds(pl.multiple_of(g * piece, piece), piece)
        for j in order:
            block_copy(g, j).wait_recv()
        sums = jnp.dot(xbuf[at, :], vectors[...], preferred_element_type=F32)
        scale = s_ref[...]
        mode = (sums[:, :rank] / scale).astype(BF16)
        push = (sums[:, rank:] / scale).astype(BF16)
        modes[at, :] = mode
        pltpu.make_async_copy(modes.at[at, :], modes_hbm.at[at, :], m_sem.at[g]).start()
        return mode, push

    def finish(g, _):
        at = pl.ds(pl.multiple_of(g * piece, piece), piece)
        for j in order:
            block_copy(g, j).wait_send()
        pltpu.make_async_copy(modes.at[at, :], modes_hbm.at[at, :], m_sem.at[g]).wait()
        return _

    contract = (((0,), (0,)), ((), ()))
    if not fused:
        (pushed, op, op_sem) = scratch[8:]

        def step(g, _):
            at = pl.ds(pl.multiple_of(g * piece, piece), piece)
            pushed[at, :] = project(g)[1]
            return _

        lax.fori_loop(0, groups, step, 0)
        op[...] = lax.dot_general(modes[...], pushed[...], contract, preferred_element_type=F32)
        out = pltpu.make_async_copy(op, op_hbm, op_sem)
        out.start()
        lax.fori_loop(0, groups, finish, 0)
        out.wait()
        return

    (stage, gathered, term, parts, whole, p_send, p_recv, p_own,
     r_send, r_recv, z_send, z_recv, w_send, f_send, w_recv, op_sem) = scratch[8:]
    tall, wide = rank // 4, rank // 2

    def share_copy(g, j):
        to = lax.rem(space + j, n_space)
        return pltpu.make_async_remote_copy(
            src_ref=stage.at[g, to],
            dst_ref=gathered.at[g, pl.ds(pl.multiple_of(space * piece, piece), piece), :],
            send_sem=p_send.at[g, j],
            recv_sem=p_recv.at[g, j],
            device_id=(to, snap),
            device_id_type=MESH,
        )

    def share_own(g):
        return pltpu.make_async_copy(
            stage.at[g, space],
            gathered.at[g, pl.ds(pl.multiple_of(space * piece, piece), piece), :],
            p_own.at[g],
        )

    def add_term(g):
        share_own(g).wait()
        for j in range(1, n_space):
            share_copy(g, j).wait_recv()
        return lax.dot_general(
            gathered[g, :, :tall], gathered[g, :, tall:], contract, preferred_element_type=F32
        )

    def step(g, _):
        mode, push = project(g)
        for p in range(n_space):
            stage[g, p, :, :tall] = mode[:, (p // 2) * tall : (p // 2 + 1) * tall]
            stage[g, p, :, tall:] = push[:, (p % 2) * wide : (p % 2 + 1) * wide]
        for j in (3, 4, 5, 2, 6, 1, 7):
            share_copy(g, j).start()
        share_own(g).start()

        @pl.when(g > 0)
        def _add():
            term[...] += add_term(g - 1)

        return _

    term[...] = jnp.zeros_like(term)
    lax.fori_loop(0, groups, step, 0)
    term[...] += add_term(groups - 1)

    slab = tall // n_snap

    def reduce_copy(j):
        to = lax.rem(snap + j, n_snap)
        return pltpu.make_async_remote_copy(
            src_ref=term.at[pl.ds(pl.multiple_of(to * slab, slab), slab), :],
            dst_ref=parts.at[j],
            send_sem=r_send.at[j],
            recv_sem=r_recv.at[j],
            device_id=(space, to),
            device_id_type=MESH,
        )

    for j in order:
        reduce_copy(j).start()
    mine = pl.multiple_of(snap * slab, slab)
    total = term[pl.ds(mine, slab), :]
    for j in order:
        reduce_copy(j).wait_recv()
    for j in order:
        total = total + parts[j]

    def place(p, start, size):
        return whole.at[
            pl.ds(pl.multiple_of((p // 2) * tall + start, size), size),
            pl.ds(pl.multiple_of(lax.rem(p, 2) * wide, wide), wide),
        ]

    parts[0] = total
    piece_at = place(space, mine, slab)
    piece_at[...] = parts[0].astype(BF16)

    def slab_copy(j):
        return pltpu.make_async_remote_copy(
            src_ref=piece_at,
            dst_ref=piece_at,
            send_sem=z_send.at[j],
            recv_sem=z_recv.at[j],
            device_id=(space, lax.rem(snap + j, n_snap)),
            device_id_type=MESH,
        )

    def slab_arrival(j):
        origin = lax.rem(snap + n_snap - j, n_snap)
        at = place(space, origin * slab, slab)
        return pltpu.make_async_remote_copy(
            src_ref=at, dst_ref=at, send_sem=z_send.at[j], recv_sem=z_recv.at[j],
            device_id=(space, lax.rem(snap + j, n_snap)), device_id_type=MESH,
        )

    for j in order:
        slab_copy(j).start()
    for j in order:
        slab_arrival(j).wait_recv()

    chip, core = space // 2, lax.rem(space, 2)
    chips = n_space // 2
    sibling = space + 1 - 2 * core

    def spread(p, to, send_sem):
        return pltpu.make_async_remote_copy(
            src_ref=place(p, 0, tall), dst_ref=place(p, 0, tall),
            send_sem=send_sem, recv_sem=w_recv.at[p],
            device_id=(to, snap), device_id_type=MESH,
        )

    def partner(j):
        return lax.rem(chip + j, chips) * 2 + core

    for j in (2, 1, 3):
        spread(space, partner(j), w_send.at[j]).start()
    spread(space, sibling, f_send.at[0]).start()
    for j in (1, 3, 2):
        came = partner(j)
        spread(came, sibling, f_send.at[j]).wait_recv()
        spread(came, sibling, f_send.at[j]).start()
    for j in range(chips):
        there = lax.rem(chip + j, chips) * 2 + 1 - core
        spread(there, sibling, f_send.at[j]).wait_recv()
    out = pltpu.make_async_copy(whole, op_hbm, op_sem)
    out.start()

    lax.fori_loop(0, groups, finish, 0)

    def finish_shares(g, _):
        for j in range(1, n_space):
            share_copy(g, j).wait_send()
        return _

    lax.fori_loop(0, groups, finish_shares, 0)
    for j in order:
        reduce_copy(j).wait_send()
        slab_copy(j).wait_send()
    for j in range(1, chips):
        spread(space, partner(j), w_send.at[j]).wait_send()
        spread(partner(j), sibling, f_send.at[j]).wait_send()
    spread(space, sibling, f_send.at[0]).wait_send()
    out.wait()


def per_device(n_space, n_snap, snapshots, eigen_vectors, singular):
    cols = snapshots.shape[1]
    rows = snapshots.shape[0] // n_snap
    snaps, rank = eigen_vectors.shape
    groups = 4
    fused = n_space == PLANE
    piece = rows // groups
    dma = pltpu.SemaphoreType.DMA
    scratch = [
        pltpu.VMEM((rows, snaps), BF16),
        pltpu.VMEM((snaps, 2 * rank), BF16),
        pltpu.VMEM((rows, rank), BF16),
        dma,
        dma((groups, n_snap)),
        dma((groups, n_snap)),
        dma,
        dma((groups,)),
    ]
    if fused:
        tall, wide = rank // 4, rank // 2
        scratch += [
            pltpu.VMEM((groups, n_space, piece, tall + wide), BF16),
            pltpu.VMEM((groups, n_space * piece, tall + wide), BF16),
            pltpu.VMEM((tall, wide), F32),
            pltpu.VMEM((n_snap, tall // n_snap, wide), F32),
            pltpu.VMEM((rank, rank), BF16),
            dma((groups, n_space)),
            dma((groups, n_space)),
            dma((groups,)),
            dma((n_snap,)),
            dma((n_snap,)),
            dma((n_snap,)),
            dma((n_snap,)),
            dma((n_space // 2,)),
            dma((n_space // 2,)),
            dma((n_space,)),
            dma,
        ]
    else:
        scratch += [pltpu.VMEM((rows, rank), BF16), pltpu.VMEM((rank, rank), F32), dma]
    anywhere = pl.BlockSpec(memory_space=pl.ANY)
    pod_modes, operator = pl.pallas_call(
        functools.partial(kernel, (n_space, n_snap, groups, fused)),
        out_shape=(
            jax.ShapeDtypeStruct((rows, rank), BF16),
            jax.ShapeDtypeStruct((rank, rank), BF16 if fused else F32),
        ),
        in_specs=[anywhere, anywhere, pl.BlockSpec(memory_space=pltpu.VMEM)],
        out_specs=(anywhere, anywhere),
        scratch_shapes=scratch,
        compiler_params=pltpu.CompilerParams(
            collective_id=0, has_side_effects=True, vmem_limit_bytes=40 * 1024 * 1024
        ),
        cost_estimate=pl.CostEstimate(
            flops=4 * rows * snaps * rank, bytes_accessed=4 * snaps * rank, transcendentals=0
        ),
    )(snapshots, eigen_vectors, singular.reshape(1, rank))
    if not fused:
        return pod_modes, lax.psum(operator, ("space", "snap"))
    return pod_modes, operator.astype(F32)


def solution(mesh):
    n_space, n_snap = mesh.shape["space"], mesh.shape["snap"]
    return jax.shard_map(
        functools.partial(per_device, n_space, n_snap),
        mesh=mesh,
        in_specs=(P("space", "snap"), P(), P()),
        out_specs=(P(("space", "snap"), None), P()),
        check_vma=False,
    )
```

```python
import functools

import jax
import jax.numpy as jnp
from jax import lax
from jax.experimental import pallas as pl
from jax.experimental.pallas import tpu as pltpu
from jax.sharding import PartitionSpec as P

MESH = pl.DeviceIdType.MESH
F32, BF16 = jnp.float32, jnp.bfloat16
DEPTH = 2
PLANE = 8


def shift_vectors(vectors, snaps, rank):
    rows = 64

    def one(i, above):
        at = pl.ds(pl.multiple_of(i * rows, rows), rows)
        chunk = vectors[at, :rank].astype(F32)
        moved = pltpu.roll(chunk, 1, 0)
        first = lax.broadcasted_iota(jnp.int32, chunk.shape, 0) == 0
        vectors[at, rank:] = jnp.where(first, above, moved).astype(BF16)
        return chunk[rows - 1 :, :]

    last = vectors[snaps - 16 :, :rank].astype(F32)[15:, :]
    lax.fori_loop(0, snaps // rows, one, last)


def kernel(sizes, x_hbm, e_hbm, s_hbm, modes_hbm, op_hbm, *scratch):
    n_space, n_snap, cuts, fused = sizes
    groups = len(cuts)
    (xbuf, vectors, modes, s_ref, e_sem, x_send, x_recv, own_sem, s_sem, m_sem) = scratch[:10]
    space, snap = lax.axis_index("space"), lax.axis_index("snap")
    rows, rank = modes.shape
    cols = x_hbm.shape[1]
    snaps = cols * n_snap
    starts = [sum(cuts[:g]) for g in range(groups)]

    load_e = pltpu.make_async_copy(e_hbm, vectors.at[:, :rank], e_sem)
    load_e.start()
    load_s = pltpu.make_async_copy(s_hbm, s_ref, s_sem)
    load_s.start()
    own = pltpu.make_async_copy(
        x_hbm.at[pl.ds(pl.multiple_of(snap * rows, rows), rows), :],
        xbuf.at[snap],
        own_sem,
    )
    own.start()

    barrier = pltpu.get_barrier_semaphore()
    for j in range(1, n_snap):
        pl.semaphore_signal(
            barrier, inc=1, device_id=(space, lax.rem(snap + j, n_snap)), device_id_type=MESH
        )
    if fused:
        for j in range(1, n_space):
            pl.semaphore_signal(
                barrier, inc=1, device_id=(lax.rem(space + j, n_space), snap), device_id_type=MESH
            )
    pl.semaphore_wait(barrier, n_snap - 1 + (n_space - 1 if fused else 0))

    def block_copy(g, j):
        to = lax.rem(snap + j, n_snap)
        return pltpu.make_async_remote_copy(
            src_ref=x_hbm.at[pl.ds(pl.multiple_of(to * rows + starts[g], 16), cuts[g]), :],
            dst_ref=xbuf.at[snap, pl.ds(starts[g], cuts[g]), :],
            send_sem=x_send.at[g, j],
            recv_sem=x_recv.at[g, j],
            device_id=(space, to),
            device_id_type=MESH,
        )

    order = sorted(range(1, n_snap), key=lambda j: -min(j, n_snap - j))

    def send_blocks(g):
        for j in order:
            block_copy(g, j).start()

    depth = min(DEPTH, groups)
    for g in range(depth):
        send_blocks(g)

    load_e.wait()
    shift_vectors(vectors, snaps, rank)
    own.wait()
    load_s.wait()

    def project(g):
        at = pl.ds(starts[g], cuts[g])
        for j in order:
            block_copy(g, j).wait_send()
        if g + depth < groups:
            send_blocks(g + depth)
        for j in order:
            block_copy(g, j).wait_recv()
        sums = jnp.dot(xbuf[0, at, :], vectors[:cols, :], preferred_element_type=F32)
        for k in range(1, n_snap):
            sums += jnp.dot(
                xbuf[k, at, :], vectors[k * cols : (k + 1) * cols, :], preferred_element_type=F32
            )
        scale = s_ref[...]
        mode = (sums[:, :rank] / scale).astype(BF16)
        push = (sums[:, rank:] / scale).astype(BF16)
        modes[at, :] = mode
        pltpu.make_async_copy(modes.at[at, :], modes_hbm.at[at, :], m_sem.at[g]).start()
        return mode, push

    def finish():
        for g in range(groups):
            at = pl.ds(starts[g], cuts[g])
            pltpu.make_async_copy(modes.at[at, :], modes_hbm.at[at, :], m_sem.at[g]).wait()

    contract = (((0,), (0,)), ((), ()))
    if not fused:
        (pushed, op, op_sem) = scratch[10:]

        for g in range(groups):
            pushed[pl.ds(starts[g], cuts[g]), :] = project(g)[1]
        op[...] = lax.dot_general(modes[...], pushed[...], contract, preferred_element_type=F32)
        out = pltpu.make_async_copy(op, op_hbm, op_sem)
        out.start()
        finish()
        out.wait()
        return

    (stage, gathered, term, parts, whole, p_send, p_recv, p_own,
     r_send, r_recv, z_send, z_recv, w_send, f_send, w_recv, op_sem) = scratch[10:]
    tall, wide = rank // 4, rank // 2

    def region(g):
        start = pl.multiple_of(n_space * starts[g] + space * cuts[g], 16)
        return gathered.at[pl.ds(start, cuts[g]), :]

    def share_copy(g, j):
        to = lax.rem(space + j, n_space)
        return pltpu.make_async_remote_copy(
            src_ref=stage.at[to, pl.ds(starts[g], cuts[g]), :],
            dst_ref=region(g),
            send_sem=p_send.at[g, j],
            recv_sem=p_recv.at[g, j],
            device_id=(to, snap),
            device_id_type=MESH,
        )

    def share_own(g):
        return pltpu.make_async_copy(
            stage.at[space, pl.ds(starts[g], cuts[g]), :], region(g), p_own.at[g]
        )

    def add_term(g):
        share_own(g).wait()
        for j in range(1, n_space):
            share_copy(g, j).wait_recv()
        at = pl.ds(n_space * starts[g], n_space * cuts[g])
        return lax.dot_general(
            gathered[at, :tall], gathered[at, tall:], contract, preferred_element_type=F32
        )

    for g in range(groups):
        mode, push = project(g)
        at = pl.ds(starts[g], cuts[g])
        for p in range(n_space):
            stage[p, at, :tall] = mode[:, (p // 2) * tall : (p // 2 + 1) * tall]
            stage[p, at, tall:] = push[:, (p % 2) * wide : (p % 2 + 1) * wide]
        for j in (3, 4, 5, 2, 6, 1, 7):
            share_copy(g, j).start()
        share_own(g).start()
        if g == 1:
            term[...] = add_term(0)
        elif g > 1:
            term[...] += add_term(g - 1)
    term[...] += add_term(groups - 1)

    slab = tall // n_snap

    def reduce_copy(j):
        to = lax.rem(snap + j, n_snap)
        return pltpu.make_async_remote_copy(
            src_ref=term.at[pl.ds(pl.multiple_of(to * slab, slab), slab), :],
            dst_ref=parts.at[j],
            send_sem=r_send.at[j],
            recv_sem=r_recv.at[j],
            device_id=(space, to),
            device_id_type=MESH,
        )

    for j in order:
        reduce_copy(j).start()
    mine = pl.multiple_of(snap * slab, slab)
    total = term[pl.ds(mine, slab), :]
    for j in order:
        reduce_copy(j).wait_recv()
    for j in order:
        total = total + parts[j]

    def place(p, start, size):
        return whole.at[
            pl.ds(pl.multiple_of((p // 2) * tall + start, size), size),
            pl.ds(pl.multiple_of(lax.rem(p, 2) * wide, wide), wide),
        ]

    parts[0] = total
    piece_at = place(space, mine, slab)
    piece_at[...] = parts[0].astype(BF16)

    def slab_copy(j):
        return pltpu.make_async_remote_copy(
            src_ref=piece_at,
            dst_ref=piece_at,
            send_sem=z_send.at[j],
            recv_sem=z_recv.at[j],
            device_id=(space, lax.rem(snap + j, n_snap)),
            device_id_type=MESH,
        )

    def slab_arrival(j):
        origin = lax.rem(snap + n_snap - j, n_snap)
        at = place(space, origin * slab, slab)
        return pltpu.make_async_remote_copy(
            src_ref=at, dst_ref=at, send_sem=z_send.at[j], recv_sem=z_recv.at[j],
            device_id=(space, lax.rem(snap + j, n_snap)), device_id_type=MESH,
        )

    chip, core = space // 2, lax.rem(space, 2)
    chips = n_space // 2
    sibling = space + 1 - 2 * core
    near = sorted(range(n_snap), key=lambda j: min(j, n_snap - j))

    def partner(i):
        return lax.rem(chip + i, chips) * 2 + core

    def spread(i, j, p, to):
        at = place(p, lax.rem(snap + n_snap - j, n_snap) * slab, slab)
        return pltpu.make_async_remote_copy(
            src_ref=at, dst_ref=at, send_sem=w_send.at[i, j], recv_sem=w_recv.at[p, j],
            device_id=(to, snap), device_id_type=MESH,
        )

    def hand_over(i, j):
        at = place(partner(i), lax.rem(snap + n_snap - j, n_snap) * slab, slab)
        return pltpu.make_async_remote_copy(
            src_ref=at, dst_ref=at, send_sem=f_send.at[i, j], recv_sem=w_recv.at[partner(i), j],
            device_id=(sibling, snap), device_id_type=MESH,
        )

    for j in order:
        slab_copy(j).start()
    for j in near:
        if j:
            slab_arrival(j).wait_recv()
        for i in (2, 1, 3):
            spread(i, j, space, partner(i)).start()
        hand_over(0, j).start()
    for j in near:
        for i in (1, 3, 2):
            hand_over(i, j).wait_recv()
            hand_over(i, j).start()
    for j in near:
        for i in range(chips):
            there = lax.rem(chip + i, chips) * 2 + 1 - core
            spread(i, j, there, sibling).wait_recv()
    out = pltpu.make_async_copy(whole, op_hbm, op_sem)
    out.start()

    finish()

    for g in range(groups):
        for j in range(1, n_space):
            share_copy(g, j).wait_send()
    for j in order:
        reduce_copy(j).wait_send()
        slab_copy(j).wait_send()
    for j in near:
        for i in range(chips):
            if i:
                spread(i, j, space, partner(i)).wait_send()
            hand_over(i, j).wait_send()
    out.wait()


def cut(rows):
    if rows % 256 == 0:
        return [share * rows // 16 for share in (5, 5, 4, 2)]
    return [rows // 4] * 4 if rows % 64 == 0 else [rows]


def per_device(n_space, n_snap, snapshots, eigen_vectors, singular):
    cols = snapshots.shape[1]
    rows = snapshots.shape[0] // n_snap
    snaps, rank = eigen_vectors.shape
    fused = n_space == PLANE
    cuts = cut(rows)
    groups = len(cuts)
    dma = pltpu.SemaphoreType.DMA
    scratch = [
        pltpu.VMEM((n_snap, rows, snaps // n_snap), BF16),
        pltpu.VMEM((snaps, 2 * rank), BF16),
        pltpu.VMEM((rows, rank), BF16),
        pltpu.VMEM((1, rank), F32),
        dma,
        dma((groups, n_snap)),
        dma((groups, n_snap)),
        dma,
        dma,
        dma((groups,)),
    ]
    if fused:
        tall, wide = rank // 4, rank // 2
        scratch += [
            pltpu.VMEM((n_space, rows, tall + wide), BF16),
            pltpu.VMEM((n_space * rows, tall + wide), BF16),
            pltpu.VMEM((tall, wide), F32),
            pltpu.VMEM((n_snap, tall // n_snap, wide), F32),
            pltpu.VMEM((rank, rank), BF16),
            dma((groups, n_space)),
            dma((groups, n_space)),
            dma((groups,)),
            dma((n_snap,)),
            dma((n_snap,)),
            dma((n_snap,)),
            dma((n_snap,)),
            dma((n_space // 2, n_snap)),
            dma((n_space // 2, n_snap)),
            dma((n_space, n_snap)),
            dma,
        ]
    else:
        scratch += [pltpu.VMEM((rows, rank), BF16), pltpu.VMEM((rank, rank), F32), dma]
    operands = (snapshots, eigen_vectors, singular.reshape(1, rank))
    in_hbm = pl.BlockSpec(memory_space=pltpu.HBM)
    pod_modes, operator = pl.pallas_call(
        functools.partial(kernel, (n_space, n_snap, cuts, fused)),
        out_shape=(
            jax.ShapeDtypeStruct((rows, rank), BF16),
            jax.ShapeDtypeStruct((rank, rank), BF16 if fused else F32),
        ),
        in_specs=[in_hbm] * 3,
        out_specs=(in_hbm, in_hbm),
        scratch_shapes=scratch,
        compiler_params=pltpu.CompilerParams(
            collective_id=0, has_side_effects=True, vmem_limit_bytes=40 * 1024 * 1024
        ),
        cost_estimate=pl.CostEstimate(
            flops=4 * rows * snaps * rank, bytes_accessed=4 * snaps * rank, transcendentals=0
        ),
    )(*[pltpu.with_memory_space_constraint(a, pltpu.HBM) for a in operands])
    if not fused:
        return pod_modes, lax.psum(operator, ("space", "snap"))
    return pod_modes, operator.astype(F32)


def solution(mesh):
    n_space, n_snap = mesh.shape["space"], mesh.shape["snap"]
    return jax.shard_map(
        functools.partial(per_device, n_space, n_snap),
        mesh=mesh,
        in_specs=(P("space", "snap"), P(), P()),
        out_specs=(P(("space", "snap"), None), P()),
        check_vma=False,
    )
```

```python
import functools

import jax
import jax.numpy as jnp
from jax import lax
from jax.experimental import pallas as pl
from jax.experimental.pallas import tpu as pltpu
from jax.sharding import PartitionSpec as P

MESH = pl.DeviceIdType.MESH
F32, BF16 = jnp.float32, jnp.bfloat16
DEPTH = 2
PLANE = 8


def shift_vectors(vectors, snaps, rank):
    rows = 64

    def one(i, above):
        at = pl.ds(pl.multiple_of(i * rows, rows), rows)
        chunk = vectors[at, :rank].astype(F32)
        moved = pltpu.roll(chunk, 1, 0)
        first = lax.broadcasted_iota(jnp.int32, chunk.shape, 0) == 0
        vectors[at, rank:] = jnp.where(first, above, moved).astype(BF16)
        return chunk[rows - 1 :, :]

    last = vectors[snaps - 16 :, :rank].astype(F32)[15:, :]
    lax.fori_loop(0, snaps // rows, one, last)


def kernel(sizes, x_hbm, e_hbm, s_hbm, modes_hbm, op_hbm, *scratch):
    n_space, n_snap, cuts, fused = sizes
    groups = len(cuts)
    (xbuf, vectors, modes, s_ref, e_sem, x_send, x_recv, own_sem, s_sem, m_sem) = scratch[:10]
    space, snap = lax.axis_index("space"), lax.axis_index("snap")
    rows, rank = modes.shape
    cols = x_hbm.shape[1]
    snaps = cols * n_snap
    starts = [sum(cuts[:g]) for g in range(groups)]

    load_e = pltpu.make_async_copy(e_hbm, vectors.at[:, :rank], e_sem)
    load_e.start()
    load_s = pltpu.make_async_copy(s_hbm, s_ref, s_sem)
    load_s.start()
    own = pltpu.make_async_copy(
        x_hbm.at[pl.ds(pl.multiple_of(snap * rows, rows), rows), :],
        xbuf.at[snap],
        own_sem,
    )
    own.start()

    barrier = pltpu.get_barrier_semaphore()
    for j in range(1, n_snap):
        pl.semaphore_signal(
            barrier, inc=1, device_id=(space, lax.rem(snap + j, n_snap)), device_id_type=MESH
        )
    if fused:
        for j in range(1, n_space):
            pl.semaphore_signal(
                barrier, inc=1, device_id=(lax.rem(space + j, n_space), snap), device_id_type=MESH
            )
    pl.semaphore_wait(barrier, n_snap - 1 + (n_space - 1 if fused else 0))

    def block_copy(g, j):
        to = lax.rem(snap + j, n_snap)
        return pltpu.make_async_remote_copy(
            src_ref=x_hbm.at[pl.ds(pl.multiple_of(to * rows + starts[g], 16), cuts[g]), :],
            dst_ref=xbuf.at[snap, pl.ds(starts[g], cuts[g]), :],
            send_sem=x_send.at[g, j],
            recv_sem=x_recv.at[g, j],
            device_id=(space, to),
            device_id_type=MESH,
        )

    order = sorted(range(1, n_snap), key=lambda j: -min(j, n_snap - j))

    def send_blocks(g):
        for j in order:
            block_copy(g, j).start()

    depth = min(DEPTH, groups)
    for g in range(depth):
        send_blocks(g)

    load_e.wait()
    shift_vectors(vectors, snaps, rank)
    own.wait()
    load_s.wait()

    def project(g):
        at = pl.ds(starts[g], cuts[g])
        for j in order:
            block_copy(g, j).wait_send()
        if g + depth < groups:
            send_blocks(g + depth)
        for j in order:
            block_copy(g, j).wait_recv()
        sums = jnp.dot(xbuf[0, at, :], vectors[:cols, :], preferred_element_type=F32)
        for k in range(1, n_snap):
            sums += jnp.dot(
                xbuf[k, at, :], vectors[k * cols : (k + 1) * cols, :], preferred_element_type=F32
            )
        scale = s_ref[...]
        mode = (sums[:, :rank] / scale).astype(BF16)
        push = (sums[:, rank:] / scale).astype(BF16)
        modes[at, :] = mode
        pltpu.make_async_copy(modes.at[at, :], modes_hbm.at[at, :], m_sem.at[g]).start()
        return mode, push

    def finish():
        for g in range(groups):
            at = pl.ds(starts[g], cuts[g])
            pltpu.make_async_copy(modes.at[at, :], modes_hbm.at[at, :], m_sem.at[g]).wait()

    contract = (((0,), (0,)), ((), ()))
    if not fused:
        (pushed, op, op_sem) = scratch[10:]

        for g in range(groups):
            pushed[pl.ds(starts[g], cuts[g]), :] = project(g)[1]
        op[...] = lax.dot_general(modes[...], pushed[...], contract, preferred_element_type=F32)
        out = pltpu.make_async_copy(op, op_hbm, op_sem)
        out.start()
        finish()
        out.wait()
        return

    (stage, gathered, term, parts, whole, p_send, p_recv, p_own,
     r_send, r_recv, z_send, z_recv, w_send, f_send, w_recv, op_sem) = scratch[10:]
    tall, wide = rank // 4, rank // 2

    def region(g):
        start = pl.multiple_of(n_space * starts[g] + space * cuts[g], 16)
        return gathered.at[pl.ds(start, cuts[g]), :]

    def share_copy(g, j):
        to = lax.rem(space + j, n_space)
        return pltpu.make_async_remote_copy(
            src_ref=stage.at[to, pl.ds(starts[g], cuts[g]), :],
            dst_ref=region(g),
            send_sem=p_send.at[g, j],
            recv_sem=p_recv.at[g, j],
            device_id=(to, snap),
            device_id_type=MESH,
        )

    def share_own(g):
        return pltpu.make_async_copy(
            stage.at[space, pl.ds(starts[g], cuts[g]), :], region(g), p_own.at[g]
        )

    def add_term(g):
        share_own(g).wait()
        for j in range(1, n_space):
            share_copy(g, j).wait_recv()
        at = pl.ds(n_space * starts[g], n_space * cuts[g])
        return lax.dot_general(
            gathered[at, :tall], gathered[at, tall:], contract, preferred_element_type=F32
        )

    for g in range(groups):
        mode, push = project(g)
        at = pl.ds(starts[g], cuts[g])
        for p in range(n_space):
            stage[p, at, :tall] = mode[:, (p // 2) * tall : (p // 2 + 1) * tall]
            stage[p, at, tall:] = push[:, (p % 2) * wide : (p % 2 + 1) * wide]
        for j in (3, 4, 5, 2, 6, 1, 7):
            share_copy(g, j).start()
        share_own(g).start()
        if g == 1:
            term[...] = add_term(0)
        elif g > 1:
            term[...] += add_term(g - 1)
    term[...] += add_term(groups - 1)

    slab = tall // n_snap

    def reduce_copy(j):
        to = lax.rem(snap + j, n_snap)
        return pltpu.make_async_remote_copy(
            src_ref=term.at[pl.ds(pl.multiple_of(to * slab, slab), slab), :],
            dst_ref=parts.at[j],
            send_sem=r_send.at[j],
            recv_sem=r_recv.at[j],
            device_id=(space, to),
            device_id_type=MESH,
        )

    for j in order:
        reduce_copy(j).start()
    mine = pl.multiple_of(snap * slab, slab)
    total = term[pl.ds(mine, slab), :]
    for j in order:
        reduce_copy(j).wait_recv()
    for j in order:
        total = total + parts[j]

    def place(p, start, size):
        return whole.at[
            pl.ds(pl.multiple_of((p // 2) * tall + start, size), size),
            pl.ds(pl.multiple_of(lax.rem(p, 2) * wide, wide), wide),
        ]

    parts[0] = total
    piece_at = place(space, mine, slab)
    piece_at[...] = parts[0].astype(BF16)

    def slab_copy(j):
        return pltpu.make_async_remote_copy(
            src_ref=piece_at,
            dst_ref=piece_at,
            send_sem=z_send.at[j],
            recv_sem=z_recv.at[j],
            device_id=(space, lax.rem(snap + j, n_snap)),
            device_id_type=MESH,
        )

    def slab_arrival(j):
        origin = lax.rem(snap + n_snap - j, n_snap)
        at = place(space, origin * slab, slab)
        return pltpu.make_async_remote_copy(
            src_ref=at, dst_ref=at, send_sem=z_send.at[j], recv_sem=z_recv.at[j],
            device_id=(space, lax.rem(snap + j, n_snap)), device_id_type=MESH,
        )

    chip, core = space // 2, lax.rem(space, 2)
    chips = n_space // 2
    sibling = space + 1 - 2 * core
    near = sorted(range(n_snap), key=lambda j: min(j, n_snap - j))

    def partner(i):
        return lax.rem(chip + i, chips) * 2 + core

    def spread(i, j, p, to):
        at = place(p, lax.rem(snap + n_snap - j, n_snap) * slab, slab)
        return pltpu.make_async_remote_copy(
            src_ref=at, dst_ref=at, send_sem=w_send.at[i, j], recv_sem=w_recv.at[p, j],
            device_id=(to, snap), device_id_type=MESH,
        )

    def hand_over(i, j):
        at = place(partner(i), lax.rem(snap + n_snap - j, n_snap) * slab, slab)
        return pltpu.make_async_remote_copy(
            src_ref=at, dst_ref=at, send_sem=f_send.at[i, j], recv_sem=w_recv.at[partner(i), j],
            device_id=(sibling, snap), device_id_type=MESH,
        )

    for j in order:
        slab_copy(j).start()
    for j in near:
        if j:
            slab_arrival(j).wait_recv()
        for i in (2, 1, 3):
            spread(i, j, space, partner(i)).start()
        hand_over(0, j).start()
    for j in near:
        for i in (1, 3, 2):
            hand_over(i, j).wait_recv()
            hand_over(i, j).start()
    for j in near:
        for i in range(chips):
            there = lax.rem(chip + i, chips) * 2 + 1 - core
            spread(i, j, there, sibling).wait_recv()
    out = pltpu.make_async_copy(whole, op_hbm, op_sem)
    out.start()

    finish()

    for g in range(groups):
        for j in range(1, n_space):
            share_copy(g, j).wait_send()
    for j in order:
        reduce_copy(j).wait_send()
        slab_copy(j).wait_send()
    for j in near:
        for i in range(chips):
            if i:
                spread(i, j, space, partner(i)).wait_send()
            hand_over(i, j).wait_send()
    out.wait()


def cut(rows):
    if rows % 256 == 0:
        return [share * rows // 16 for share in (2, 4, 4, 4, 2)]
    return [rows // 4] * 4 if rows % 64 == 0 else [rows]


def per_device(n_space, n_snap, snapshots, eigen_vectors, singular):
    cols = snapshots.shape[1]
    rows = snapshots.shape[0] // n_snap
    snaps, rank = eigen_vectors.shape
    fused = n_space == PLANE
    cuts = cut(rows)
    groups = len(cuts)
    dma = pltpu.SemaphoreType.DMA
    scratch = [
        pltpu.VMEM((n_snap, rows, snaps // n_snap), BF16),
        pltpu.VMEM((snaps, 2 * rank), BF16),
        pltpu.VMEM((rows, rank), BF16),
        pltpu.VMEM((1, rank), F32),
        dma,
        dma((groups, n_snap)),
        dma((groups, n_snap)),
        dma,
        dma,
        dma((groups,)),
    ]
    if fused:
        tall, wide = rank // 4, rank // 2
        scratch += [
            pltpu.VMEM((n_space, rows, tall + wide), BF16),
            pltpu.VMEM((n_space * rows, tall + wide), BF16),
            pltpu.VMEM((tall, wide), F32),
            pltpu.VMEM((n_snap, tall // n_snap, wide), F32),
            pltpu.VMEM((rank, rank), BF16),
            dma((groups, n_space)),
            dma((groups, n_space)),
            dma((groups,)),
            dma((n_snap,)),
            dma((n_snap,)),
            dma((n_snap,)),
            dma((n_snap,)),
            dma((n_space // 2, n_snap)),
            dma((n_space // 2, n_snap)),
            dma((n_space, n_snap)),
            dma,
        ]
    else:
        scratch += [pltpu.VMEM((rows, rank), BF16), pltpu.VMEM((rank, rank), F32), dma]
    operands = (snapshots, eigen_vectors, singular.reshape(1, rank))
    in_hbm = pl.BlockSpec(memory_space=pltpu.HBM)
    pod_modes, operator = pl.pallas_call(
        functools.partial(kernel, (n_space, n_snap, cuts, fused)),
        out_shape=(
            jax.ShapeDtypeStruct((rows, rank), BF16),
            jax.ShapeDtypeStruct((rank, rank), BF16 if fused else F32),
        ),
        in_specs=[in_hbm] * 3,
        out_specs=(in_hbm, in_hbm),
        scratch_shapes=scratch,
        compiler_params=pltpu.CompilerParams(
            collective_id=0, has_side_effects=True, vmem_limit_bytes=40 * 1024 * 1024
        ),
        cost_estimate=pl.CostEstimate(
            flops=4 * rows * snaps * rank, bytes_accessed=4 * snaps * rank, transcendentals=0
        ),
    )(*[pltpu.with_memory_space_constraint(a, pltpu.HBM) for a in operands])
    if not fused:
        return pod_modes, lax.psum(operator, ("space", "snap"))
    return pod_modes, operator.astype(F32)


def solution(mesh):
    n_space, n_snap = mesh.shape["space"], mesh.shape["snap"]
    return jax.shard_map(
        functools.partial(per_device, n_space, n_snap),
        mesh=mesh,
        in_specs=(P("space", "snap"), P(), P()),
        out_specs=(P(("space", "snap"), None), P()),
        check_vma=False,
    )
```
